1024 devices in a mesh: dp: 32 (over z_lo, x), expert: 32 (over z_hi, y, core).
Axes of the slice: x: 4, y: 4, z: 32 (z_hi: 4, z_lo: 8; z = z_hi * 8 + z_lo), core: 2. Of those that a mesh axis runs over, the one named last changes fastest.
Arguments:
- out_grad: bfloat16 [131072, 4096], P(('dp', 'expert')), may hold values from -6 to 6
- expert_ids: int32 [131072, 1], P(('dp', 'expert')), may hold values from 0 to 31; in each aligned block of 128 rows (0 to 127, 128 to 255, ...) at most 6 rows name the same one
- gate_values: bfloat16 [131072, 1], P(('dp', 'expert')), may hold values from 0.19921875 to 1
- down_weight: bfloat16 [32, 4096, 768], P('expert'), may hold values from -0.21875 to 0.21875
- gate_up: bfloat16 [32, 32, 192, 1536], P('dp', 'expert'), may hold values from -6 to 6
Outputs:
- weight_grad: bfloat16 [32, 4096, 768], P('expert', 'dp')
- gate_up_grad: bfloat16 [32, 32, 192, 1536], P('dp', 'expert')
- gate_grad: float32 [131072, 1], P(('dp', 'expert'))
The draws below stay inside these ranges and needn't reach their ends.
Inputs may be any that keep to these rules, and one draw needn't show every extreme that they name: `expert_ids`: within the 128 tokens of one device (aligned blocks of rows), no expert is named more than 6 times; some block names some expert exactly 6 times.
All inputs are finite; a program needn't handle non-finite values.
Results may differ from the reference program's by a relative error of at most 0.0057.
Values may be sent and summed in bfloat16 or wider, within the bound.
No kernel may reach another device: no remote copies, remote signals or barrier semaphores. Data moves between devices by JAX's collectives and lax.ppermute only.
A program may use at most 64 MiB of HBM per device.

```python
import math
import jax
import jax.numpy as jnp
import numpy as np
from jax import lax

D = 4096
FFW = 768
TOK_DEV = 128
TOPW = 1
EXPERTS = 32
CAP = 6
SLOTS = 192
GROUPS = 32
TOKENS = 131072
N_EXPERT = 32


def strengthened(values, rng, source, target, blocks, factor):
    def block_of(axis_at):
        return (jnp.arange(values.shape[axis_at]) // (values.shape[axis_at] // blocks)).reshape((-1,) + (1,) * (values.ndim - 1 - axis_at))

    first = jax.random.permutation(rng, blocks)[block_of(target)]
    second = (block_of(target) + blocks // 2) % blocks
    return jnp.where((block_of(source) == first) | (block_of(source) == second), factor * values, values)


def level_of(stream_key, extent, shards, least, high):
    def one(axis_at, shards_of):
        heights = jax.random.uniform(jax.random.fold_in(jax.random.fold_in(stream_key, 6), axis_at), (shards_of,), jnp.float32, least / len(shards), high / len(shards))
        return jnp.repeat(jnp.exp(heights), extent[axis_at] // shards_of).reshape((-1,) + (1,) * (len(extent) - axis_at - 1))

    factor_of = one(*shards[0])
    for cut in shards[1:]:
        factor_of = factor_of * one(*cut)
    return factor_of


def routed_block(rng, own, number, rows, count, top, bound, slope):
    order = jax.random.permutation(rng, count)
    heavy_load, common = portions_of(count, rows * top, bound, slope, True), portions_of(count, rows * top, bound, slope, False)
    places = jnp.arange(count)

    def named(sizes, offset_by):
        used = int((sizes > 0).sum())
        fixed = max(1, used // 4)
        passed = fixed + (places - fixed + offset_by * (used - fixed)) % max(1, count - fixed)
        return jnp.zeros((count,), jnp.int32).at[order[jnp.where(places < fixed, places, passed)]].set(jnp.asarray(sizes, jnp.int32))

    sizes = jnp.where(number % 4 == 0, named(heavy_load, number // 4), named(common, number - number // 4 - 1))
    mixed = jax.random.permutation(jax.random.fold_in(own, 3), count)
    donor, sink = mixed[0:count // 2 * 2:2], mixed[1:count // 2 * 2:2]
    room = jnp.minimum(sizes[donor] - 1, bound - sizes[sink]) // 2
    room = jnp.where((donor == order[0]) | (sink == order[0]) | (sizes[sink] == 0), 0, jnp.maximum(room, 0))
    passed = jax.random.randint(jax.random.fold_in(own, 4), (count // 2,), 0, 1 << 20) % (room + 1)
    sizes = sizes.at[donor].add(-passed).at[sink].add(passed)
    items = jnp.searchsorted(jnp.cumsum(sizes), jnp.arange(rows * top), side="right").astype(jnp.int32)
    grid = items.reshape(top, rows).T
    grid = grid[jax.random.permutation(jax.random.fold_in(own, 1), rows)]
    offset_by = jax.random.randint(jax.random.fold_in(own, 2), (rows, 1), 0, top)
    return jnp.take_along_axis(grid, (jnp.arange(top)[None, :] + offset_by) % top, axis=1)


def portions_of(count, total, limit, lean, full):
    weights = [(1 << 20) // math.isqrt(standing ** lean) + 1 for standing in range(1, count + 1)]
    largest = limit if full else min(limit, max(-(-total // count), total * weights[0] // sum(weights)))
    least = 1 if total - largest >= count - 1 else 0
    counts, rest = [largest] + [least] * (count - 1), total - largest - least * (count - 1)
    while rest > 0:
        free = [i for i in range(1, count) if counts[i] < largest] or [i for i in range(1, count) if counts[i] < limit]
        pool, remaining = sum([weights[i] for i in free]), rest
        for i in free:
            addition = min(limit - counts[i], max(1, remaining * weights[i] // pool), rest)
            counts[i] = counts[i] + addition
            rest = rest - addition
    return np.array(counts)


def bell_draw(own_key, dims, spread, limit, pieces=(), held_as=jnp.bfloat16):
    loudness = level_of(own_key, dims, pieces, -0.22, 0.18) if pieces else 1.0
    values = jax.random.normal(own_key, dims, jnp.float32) * spread * loudness
    return jnp.minimum(jnp.maximum(values, -limit), limit).astype(held_as)


def noise_with(rng, dims, scale, most, split, heavy, kind=jnp.bfloat16):
    entries = scale * jax.random.normal(rng, dims, jnp.float32)
    if split:
        entries = entries * level_of(rng, dims, split, -0.22, 0.18)
    return jnp.clip(strengthened(entries, jax.random.fold_in(rng, 3), *heavy), -most, most).astype(kind)


def setup_inputs(seed: int = 0) -> dict:
    keys = jax.random.split(jax.random.key(seed), 6)
    out_grad = noise_with(keys[0], (TOKENS, D), 0.2, 6.0, ((0, 1024),), (0, 1, 1024, 6.0))
    expert_ids_keys = jax.random.split(jax.random.fold_in(keys[1], 1), TOKENS // TOK_DEV)
    expert_ids_turns = jax.random.permutation(jax.random.fold_in(keys[1], 3), TOKENS // TOK_DEV)
    expert_ids = jax.vmap(lambda own, number: routed_block(jax.random.fold_in(keys[1], 2), own, number, TOK_DEV, EXPERTS, TOPW, CAP, 1))(expert_ids_keys, expert_ids_turns).reshape((TOKENS, TOPW))
    gate_values = jnp.clip(0.19921875 + 0.80078125 * jax.random.uniform(keys[2], (TOKENS, TOPW), jnp.float32) ** level_of(keys[2], (TOKENS, TOPW), ((0, 1024),), -0.2, 0.2), 0.19921875, 1.0).astype(jnp.bfloat16)
    down_weight = bell_draw(keys[3], (EXPERTS, D, FFW), FFW ** -0.5, 0.21875, ((0, 32),))
    gate_up = bell_draw(keys[4], (GROUPS, EXPERTS, SLOTS, 2 * FFW), 1.0, 6.0, ((0, 32), (1, 32)))
    return dict(out_grad=out_grad, expert_ids=expert_ids, gate_values=gate_values, down_weight=down_weight, gate_up=gate_up)


def slot_places(chosen):
    pair_count = N_EXPERT * TOK_DEV * TOPW
    source_of = jnp.arange(pair_count, dtype=jnp.int32) // (TOK_DEV * TOPW)
    onehot = (chosen[:, None] == jnp.arange(EXPERTS, dtype=jnp.int32)[None, :]).astype(jnp.int32)
    blocks = onehot.reshape(N_EXPERT, TOK_DEV * TOPW, EXPERTS)
    before = (jnp.cumsum(blocks, axis=1) - blocks).reshape(pair_count, EXPERTS)
    position = jnp.sum(before * onehot, axis=1)
    return chosen * SLOTS + source_of * CAP + position


def reference(out_grad, expert_ids, gate_values, down_weight, gate_up):
    model_width = out_grad.shape[1]
    per_group = N_EXPERT * TOK_DEV
    weight_wide = down_weight.astype(jnp.float32)

    def one_group(running, group_index):
        begin_row = (group_index * per_group).astype(jnp.int32)
        group_rows = lax.dynamic_slice_in_dim(out_grad, begin_row, per_group, 0)
        chosen = lax.dynamic_slice_in_dim(expert_ids, begin_row, per_group, 0).reshape(-1)
        group_gates = lax.dynamic_slice_in_dim(gate_values, begin_row, per_group, 0).reshape(-1)
        saved_acts = lax.dynamic_index_in_dim(gate_up, group_index, 0, keepdims=False)
        places = slot_places(chosen)
        token_of = jnp.arange(per_group * TOPW, dtype=jnp.int32) // TOPW
        received = jnp.zeros((EXPERTS * SLOTS, model_width), jnp.bfloat16).at[places].set(group_rows[token_of])
        received = received.reshape(EXPERTS, SLOTS, model_width)
        route_gate = jnp.zeros((EXPERTS * SLOTS,), jnp.bfloat16).at[places].set(group_gates)
        gates_wide = route_gate.reshape(EXPERTS, SLOTS, 1).astype(jnp.float32)
        received_wide = received.astype(jnp.float32)
        scaled = (gates_wide * received_wide).astype(jnp.bfloat16)
        gate_act = saved_acts[..., :FFW].astype(jnp.float32)
        up_act = saved_acts[..., FFW:].astype(jnp.float32)
        sigmoid_val = jax.nn.sigmoid(gate_act)
        silu_val = gate_act * sigmoid_val
        hidden = (silu_val * up_act).astype(jnp.bfloat16)
        hidden_wide = hidden.astype(jnp.float32)
        partial_term = jnp.einsum("esd,esf->edf", scaled.astype(jnp.float32), hidden_wide)
        raw_grad = jnp.einsum("esd,edf->esf", received_wide, weight_wide)
        hidden_grad = gates_wide * raw_grad
        gate_part = hidden_grad * up_act * sigmoid_val * (1.0 + gate_act * (1.0 - sigmoid_val))
        up_part = hidden_grad * silu_val
        gu_grad = jnp.concatenate([gate_part, up_part], axis=-1).astype(jnp.bfloat16)
        outputs = jnp.einsum("esf,edf->esd", hidden_wide, weight_wide)
        score = jnp.sum(received_wide * outputs, axis=-1).reshape(-1)
        route_grad = score[places].reshape(per_group, TOPW)
        return running + partial_term, (gu_grad, route_grad)

    start_sum = jnp.zeros((EXPERTS, D, FFW), jnp.float32)
    total, (gu_all, route_all) = lax.scan(one_group, start_sum, jnp.arange(GROUPS, dtype=jnp.int32))
    return total.astype(jnp.bfloat16), gu_all, route_all.reshape(-1, TOPW)
```

```python
import jax
import jax.numpy as jnp
from jax import lax
from jax.experimental import pallas as pl
from jax.experimental.pallas import tpu as pltpu
from jax.sharding import Mesh
from jax.sharding import PartitionSpec as P

BF16, F32, I32 = jnp.bfloat16, jnp.float32, jnp.int32
ZL, X, ZH, Y, C = 8, 4, 4, 4, 2
E = ZH * Y * C
CAP = 6
TOK = 128
D = 4096
LANES = 128
EXPERT = ("zh", "y", "c")
BLOCK = ZL * CAP
FAN = X * E
ROWS = FAN * CAP
SUB = 16
VMEM = 48 * 1024 * 1024


def pack_kernel(ids_ref, gate_ref, grad_ref, rows_ref, gates_ref, keys, grads):
    ids = ids_ref[...]
    onehot = (lax.broadcasted_iota(I32, (E, TOK), 0) == ids).astype(F32)
    earlier = lax.broadcasted_iota(I32, (TOK, TOK), 0) < lax.broadcasted_iota(I32, (TOK, TOK), 1)
    before = jnp.dot(onehot.astype(BF16), earlier.astype(BF16), preferred_element_type=F32)
    place = jnp.sum(before * onehot, axis=0, keepdims=True).astype(I32)
    line = lax.broadcasted_iota(I32, (E * 8, TOK), 0)
    hit = (line // 8 == ids) & (line % 8 == place)
    picked = jnp.where(hit, gate_ref[...].astype(F32), 0.0).astype(BF16)
    gates_ref[...] = jnp.dot(picked, jnp.ones((TOK, LANES), BF16), preferred_element_type=F32).astype(BF16)
    base = ids * BLOCK + place
    for z in range(ZL):
        keys[:, z * TOK : (z + 1) * TOK] = base + z * CAP
        grads[z * TOK : (z + 1) * TOK, :] = grad_ref[:, z * (X * LANES) : (z + 1) * (X * LANES)]
    step = 8 * BLOCK

    def body(i, carry):
        row = lax.broadcasted_iota(I32, (step, ZL * TOK), 0) + i * step
        take = jnp.where(row == keys[...], 1.0, 0.0).astype(BF16)
        out = jnp.dot(take, grads[...], preferred_element_type=F32).astype(BF16)
        for q in range(X):
            rows_ref[q, pl.ds(pl.multiple_of(i * step, step), step), :] = out[:, q * LANES : (q + 1) * LANES]
        return carry

    lax.fori_loop(0, E * BLOCK // step, body, 0)


def pack(ids, gates, grad):
    return pl.pallas_call(
        pack_kernel,
        out_shape=(
            jax.ShapeDtypeStruct((X, E * BLOCK, LANES), BF16),
            jax.ShapeDtypeStruct((E * 8, LANES), BF16),
        ),
        scratch_shapes=[pltpu.VMEM((1, ZL * TOK), I32), pltpu.VMEM((ZL * TOK, X * LANES), BF16)],
        compiler_params=pltpu.CompilerParams(vmem_limit_bytes=VMEM),
        cost_estimate=pl.CostEstimate(flops=2 * E * BLOCK * ZL * TOK * X * LANES, bytes_accessed=3 << 20, transcendentals=0),
        name="pack",
    )(ids, gates, grad)


def weight_kernel(recv_ref, acts_ref, part_ref, plain_ref, scaled):
    chunks = FAN // SUB
    size = SUB * BLOCK
    group = SUB * CAP
    out = lax.broadcasted_iota(I32, (size, size), 0)
    col = lax.broadcasted_iota(I32, (size, size), 1)
    inner = out % group
    source = (inner // CAP) * BLOCK + (out // group) * CAP + inner % CAP
    order = jnp.where(source == col, 1.0, 0.0).astype(BF16)
    for k in range(chunks):
        sorted_rows = jnp.dot(order, recv_ref[k], preferred_element_type=F32)
        gate = acts_ref[k * group : (k + 1) * group, 768:].astype(F32)
        for z in range(ZL):
            tile = sorted_rows[z * group : (z + 1) * group, :]
            plain_ref[k * group : (k + 1) * group, z * LANES : (z + 1) * LANES] = tile.astype(BF16)
            scaled[k * group : (k + 1) * group, z * LANES : (z + 1) * LANES] = (tile * gate).astype(BF16)
    part_ref[...] = lax.dot_general(
        scaled[...], acts_ref[:, :768], (((0,), (0,)), ((), ())), preferred_element_type=F32
    ).astype(part_ref.dtype)


def weight_part(recv, acts):
    return pl.pallas_call(
        weight_kernel,
        out_shape=(
            jax.ShapeDtypeStruct((ZL * LANES, 768), F32),
            jax.ShapeDtypeStruct((ROWS, ZL * LANES), BF16),
        ),
        scratch_shapes=[pltpu.VMEM((ROWS, ZL * LANES), BF16)],
        compiler_params=pltpu.CompilerParams(vmem_limit_bytes=VMEM),
        cost_estimate=pl.CostEstimate(flops=4 * ROWS * ROWS * ZL * LANES, bytes_accessed=8 << 20, transcendentals=0),
        name="weight_part",
    )(recv, acts)


def cycle(parts, own, n):
    turned = [parts[(n - k) % n] for k in range(n)]
    return lax.dynamic_slice_in_dim(jnp.stack(turned + turned), (n - own) % n, n, 0)


def spread(blocks, axis, n, dim):
    own = lax.axis_index(axis)
    parts = [lax.dynamic_index_in_dim(blocks, own, dim, keepdims=False)]
    for d in range(1, n):
        block = lax.dynamic_index_in_dim(blocks, (own + d) % n, dim, keepdims=False)
        parts.append(lax.ppermute(block, axis, [(i, (i + d) % n) for i in range(n)]))
    return cycle(parts, own, n)


def per_device(out_grad, expert_ids, gate_values, down_weight, gate_up):
    own_x = lax.axis_index("x")
    rows, gates = pack(expert_ids.reshape(1, TOK), gate_values.reshape(1, TOK), out_grad)
    recv = lax.all_to_all(
        rows.reshape(FAN, BLOCK, LANES), ("x",) + EXPERT, split_axis=0, concat_axis=0, tiled=True
    )
    g = spread(gates.reshape(ZH, Y, C, 8, LANES), "c", C, 2)
    g = spread(g, "y", Y, 2)
    g = spread(g, "zh", ZH, 2)
    gate_slots = g[..., :CAP, :].reshape(E * CAP, LANES)

    saved = gate_up[0, 0]
    gate_act = saved[:, :768].astype(F32)
    up_act = saved[:, 768:].astype(F32)
    sigmoid_val = jax.nn.sigmoid(gate_act)
    silu_val = gate_act * sigmoid_val
    hidden = (silu_val * up_act).astype(BF16)
    acts = lax.all_gather(jnp.concatenate([hidden, gate_slots], axis=1), "x", axis=0, tiled=True)

    part, plain = weight_part(recv.reshape(FAN // SUB, SUB * BLOCK, LANES), acts)
    share = lax.psum_scatter(part, "zl", scatter_dimension=0, tiled=True)
    weight_share = share.astype(BF16)

    weight = lax.dynamic_index_in_dim(down_weight.reshape(ZL, X, LANES, 768), own_x, 1, keepdims=False)
    raw_part = jnp.dot(plain, weight.reshape(ZL * LANES, 768), preferred_element_type=F32).astype(BF16)
    raw_parts = lax.all_to_all(
        raw_part.reshape(X, E * CAP, 768), "x", split_axis=0, concat_axis=0, tiled=True
    )
    raw_grad = jnp.sum(raw_parts.astype(F32), axis=0)
    hidden_grad = gate_slots[:, :1].astype(F32) * raw_grad
    gate_part = hidden_grad * up_act * sigmoid_val * (1.0 + gate_act * (1.0 - sigmoid_val))
    up_part = hidden_grad * silu_val
    gu_grad = jnp.concatenate([gate_part, up_part], axis=1).astype(BF16)
    score = jnp.sum(hidden.astype(F32) * raw_grad, axis=1)
    returned = lax.all_to_all(score.reshape(E, CAP), EXPERT, split_axis=0, concat_axis=0, tiled=True)

    chosen = expert_ids.reshape(TOK)
    onehot = (chosen[:, None] == jnp.arange(E, dtype=I32)[None, :]).astype(F32)
    later = jnp.arange(TOK)[:, None] > jnp.arange(TOK)[None, :]
    before = jnp.dot(later.astype(BF16), onehot.astype(BF16), preferred_element_type=F32)
    position = jnp.sum(before * onehot, axis=1).astype(I32)
    slots = chosen * CAP + position
    hit = slots[:, None] == jnp.arange(E * CAP, dtype=I32)[None, :]
    route_grad = jnp.sum(jnp.where(hit, returned.reshape(1, E * CAP), 0.0), axis=1)
    return (weight_share[None], gu_grad[None, None], route_grad.reshape(TOK, 1))


def solution(mesh):
    fine = Mesh(mesh.devices.reshape(ZL, X, ZH, Y, C), ("zl", "x", "zh", "y", "c"))
    dp = ("zl", "x")
    return jax.shard_map(
        per_device,
        mesh=fine,
        in_specs=(
            P(dp + EXPERT, None),
            P(dp + EXPERT, None),
            P(dp + EXPERT, None),
            P(EXPERT, None, None),
            P(dp, EXPERT, None, None),
        ),
        out_specs=(
            P(EXPERT, dp, None),
            P(dp, EXPERT, None, None),
            P(dp + EXPERT, None),
        ),
        check_vma=False,
    )
```

```python
import jax
import jax.numpy as jnp
from jax import lax
from jax.experimental import pallas as pl
from jax.experimental.pallas import tpu as pltpu
from jax.sharding import Mesh
from jax.sharding import PartitionSpec as P

BF16, F32, I32 = jnp.bfloat16, jnp.float32, jnp.int32
ZL, X, ZH, Y, C = 8, 4, 4, 4, 2
E = ZH * Y * C
CAP = 6
TOK = 128
FFW = 768
LANES = 128
EXPERT = ("zh", "y", "c")
BLOCK = ZL * CAP
FAN = X * E
SLOTS = E * CAP
ROWS = X * SLOTS
WIDE = ZL * LANES
SUB = 16
VMEM = 24 * 1024 * 1024


def pack_kernel(ids_ref, gate_ref, grad_ref, rows_ref, keys, gates, grads):
    ids = ids_ref[...]
    onehot = (lax.broadcasted_iota(I32, (E, TOK), 0) == ids).astype(F32)
    earlier = lax.broadcasted_iota(I32, (TOK, TOK), 0) < lax.broadcasted_iota(I32, (TOK, TOK), 1)
    before = jnp.dot(onehot.astype(BF16), earlier.astype(BF16), preferred_element_type=F32)
    place = jnp.sum(before * onehot, axis=0, keepdims=True).astype(I32)
    base = ids * BLOCK + place
    for z in range(ZL):
        keys[:, z * TOK : (z + 1) * TOK] = base + z * CAP
        gates[:, z * TOK : (z + 1) * TOK] = gate_ref[...].astype(F32)
        grads[z * TOK : (z + 1) * TOK, :] = grad_ref[:, z * (X * LANES) : (z + 1) * (X * LANES)]
    step = 8 * BLOCK

    def body(i, carry):
        row = lax.broadcasted_iota(I32, (step, ZL * TOK), 0) + i * step
        take = jnp.where(row == keys[...], gates[...], 0.0).astype(BF16)
        out = jnp.dot(take, grads[...], preferred_element_type=F32).astype(BF16)
        for q in range(X):
            rows_ref[q, pl.ds(pl.multiple_of(i * step, step), step), :] = out[:, q * LANES : (q + 1) * LANES]
        return carry

    lax.fori_loop(0, E * BLOCK // step, body, 0)


def pack(ids, gates, grad):
    return pl.pallas_call(
        pack_kernel,
        out_shape=jax.ShapeDtypeStruct((X, E * BLOCK, LANES), BF16),
        scratch_shapes=[
            pltpu.VMEM((1, ZL * TOK), I32),
            pltpu.VMEM((1, ZL * TOK), F32),
            pltpu.VMEM((ZL * TOK, X * LANES), BF16),
        ],
        compiler_params=pltpu.CompilerParams(vmem_limit_bytes=VMEM),
        cost_estimate=pl.CostEstimate(flops=2 * E * BLOCK * ZL * TOK * X * LANES, bytes_accessed=3 << 20, transcendentals=0),
        name="pack",
    )(ids, gates, grad)


def weight_kernel(recv_ref, acts_ref, *outs):
    part_ref, scaled_ref = outs
    size = SUB * BLOCK
    group = SUB * CAP
    out = lax.broadcasted_iota(I32, (size, size), 0)
    col = lax.broadcasted_iota(I32, (size, size), 1)
    inner = out % group
    source = (inner // CAP) * BLOCK + (out // group) * CAP + inner % CAP
    order = jnp.where(source == col, 1.0, 0.0).astype(BF16)
    for k in range(FAN // SUB):
        rows = jnp.dot(order, recv_ref[k], preferred_element_type=F32).astype(BF16)
        for z in range(ZL):
            at = z * LANES
            scaled_ref[k * group : (k + 1) * group, at : at + LANES] = rows[z * group : (z + 1) * group, :]
    part_ref[...] = lax.dot_general(
        scaled_ref[...], acts_ref[...], (((0,), (0,)), ((), ())), preferred_element_type=F32
    ).astype(BF16)


def weight_part(recv, acts):
    return pl.pallas_call(
        weight_kernel,
        out_shape=(
            jax.ShapeDtypeStruct((WIDE, FFW), BF16),
            jax.ShapeDtypeStruct((ROWS, WIDE), BF16),
        ),
        compiler_params=pltpu.CompilerParams(vmem_limit_bytes=VMEM),
        cost_estimate=pl.CostEstimate(flops=4 * ROWS * ROWS * WIDE, bytes_accessed=6 << 20, transcendentals=0),
        name="weight_part",
    )(recv, acts)


def act_kernel(own_ref, scaled_ref, weight_ref, acts_ref, *outs):
    parts, score_ref, grad = outs[:X], outs[X], outs[X + 1]
    grad[...] = jnp.dot(scaled_ref[...], weight_ref[...], preferred_element_type=F32)
    for d in range(X):
        at = pl.multiple_of(lax.rem(own_ref[0] + d, X) * SLOTS, SLOTS)
        parts[d][...] = grad[pl.ds(at, SLOTS), :].astype(BF16)
    narrow = jnp.zeros((ROWS, LANES), F32)
    for f in range(0, FFW, LANES):
        narrow = narrow + grad[:, f : f + LANES] * acts_ref[:, f : f + LANES].astype(F32)
    score_ref[...] = jnp.sum(narrow.T, axis=0, keepdims=True)


def act_part(own, scaled, weight, acts):
    vmem = pl.BlockSpec(memory_space=pltpu.VMEM)
    return pl.pallas_call(
        act_kernel,
        in_specs=[pl.BlockSpec(memory_space=pltpu.SMEM), vmem, vmem, vmem],
        out_shape=[jax.ShapeDtypeStruct((SLOTS, FFW), BF16)] * X + [jax.ShapeDtypeStruct((1, ROWS), F32)],
        scratch_shapes=[pltpu.VMEM((ROWS, FFW), F32)],
        compiler_params=pltpu.CompilerParams(vmem_limit_bytes=VMEM),
        cost_estimate=pl.CostEstimate(flops=2 * ROWS * FFW * WIDE, bytes_accessed=6 << 20, transcendentals=0),
        name="act_part",
    )(own, scaled, weight, acts)


def shift(block, axis, n, d):
    return lax.ppermute(block, axis, [(i, (i + d) % n) for i in range(n)])


def per_device(out_grad, expert_ids, gate_values, down_weight, gate_up):
    own_x = lax.axis_index("x")
    rows = pack(expert_ids.reshape(1, TOK), gate_values.reshape(1, TOK), out_grad)
    recv = lax.all_to_all(
        rows.reshape(FAN, BLOCK, LANES), ("x",) + EXPERT, split_axis=0, concat_axis=0, tiled=True
    )

    saved = gate_up[0, 0]
    gate_act = saved[:, :FFW].astype(F32)
    up_act = saved[:, FFW:].astype(F32)
    sigmoid_val = jax.nn.sigmoid(gate_act)
    silu_val = gate_act * sigmoid_val
    hidden = (silu_val * up_act).astype(BF16)
    weight = lax.dynamic_index_in_dim(down_weight.reshape(ZL, X, LANES, FFW), own_x, 1, keepdims=False)
    weight = weight.reshape(WIDE, FFW)
    chosen = expert_ids.reshape(TOK)
    onehot = (chosen[:, None] == jnp.arange(E, dtype=I32)[None, :]).astype(F32)
    later = jnp.arange(TOK)[:, None] > jnp.arange(TOK)[None, :]
    before = jnp.dot(later.astype(BF16), onehot.astype(BF16), preferred_element_type=F32)
    slots = chosen * CAP + jnp.sum(before * onehot, axis=1).astype(I32)
    hidden, weight, slots = lax.optimization_barrier((hidden, weight, slots))
    came = [hidden] + [shift(hidden, "x", X, d) for d in range(1, X)]
    turned = [came[-k % X] for k in range(X)]
    acts = lax.dynamic_slice_in_dim(jnp.concatenate(turned + turned), (X - own_x) % X * SLOTS, ROWS, 0)

    part, scaled = weight_part(recv.reshape(FAN // SUB, SUB * BLOCK, LANES), acts)
    weight_share = lax.psum_scatter(part, "zl", scatter_dimension=0, tiled=True)

    *parts, score = act_part(own_x.reshape(1), scaled, weight, acts)
    returned = lax.all_to_all(
        score.reshape(FAN, 1, CAP), ("x",) + EXPERT, split_axis=0, concat_axis=0, tiled=True
    )
    hidden_grad = parts[0].astype(F32)
    for d in range(1, X):
        hidden_grad = hidden_grad + shift(parts[d], "x", X, d).astype(F32)
    gate_part = hidden_grad * up_act * sigmoid_val * (1.0 + gate_act * (1.0 - sigmoid_val))
    up_part = hidden_grad * silu_val
    gu_grad = jnp.concatenate([gate_part, up_part], axis=1).astype(BF16)

    returned = jnp.sum(returned.reshape(X, SLOTS), axis=0)
    hit = slots[:, None] == jnp.arange(SLOTS, dtype=I32)[None, :]
    route = jnp.sum(jnp.where(hit, returned[None, :], 0.0), axis=1)
    route_grad = route.reshape(TOK, 1) / gate_values.astype(F32)
    return (weight_share[None], gu_grad[None, None], route_grad)


def solution(mesh):
    fine = Mesh(mesh.devices.reshape(ZL, X, ZH, Y, C), ("zl", "x", "zh", "y", "c"))
    dp = ("zl", "x")
    return jax.shard_map(
        per_device,
        mesh=fine,
        in_specs=(
            P(dp + EXPERT, None),
            P(dp + EXPERT, None),
            P(dp + EXPERT, None),
            P(EXPERT, None, None),
            P(dp, EXPERT, None, None),
        ),
        out_specs=(
            P(EXPERT, dp, None),
            P(dp, EXPERT, None, None),
            P(dp + EXPERT, None),
        ),
        check_vma=False,
    )
```

```python
import jax
import jax.numpy as jnp
from jax import lax
from jax.experimental import pallas as pl
from jax.experimental.pallas import tpu as pltpu
from jax.sharding import Mesh
from jax.sharding import PartitionSpec as P

BF16, F32, I32 = jnp.bfloat16, jnp.float32, jnp.int32
ZA, ZB, X, ZH, Y, C = 2, 4, 4, 4, 4, 2
ZL = ZA * ZB
E = ZH * Y * C
CAP = 6
TOK = 128
FFW = 768
LANES = 128
EXPERT = ("zh", "y", "c")
BLOCK = ZL * CAP
FAN = X * E
SLOTS = E * CAP
ROWS = X * SLOTS
WIDE = ZL * LANES
SUB = 16
VMEM = 24 * 1024 * 1024


def pack_kernel(ids_ref, gate_ref, grad_ref, rows_ref, keys, gates, grads):
    ids = ids_ref[...]
    onehot = (lax.broadcasted_iota(I32, (E, TOK), 0) == ids).astype(F32)
    earlier = lax.broadcasted_iota(I32, (TOK, TOK), 0) < lax.broadcasted_iota(I32, (TOK, TOK), 1)
    before = jnp.dot(onehot.astype(BF16), earlier.astype(BF16), preferred_element_type=F32)
    place = jnp.sum(before * onehot, axis=0, keepdims=True).astype(I32)
    base = ids * BLOCK + place
    for z in range(ZL):
        keys[:, z * TOK : (z + 1) * TOK] = base + z * CAP
        gates[:, z * TOK : (z + 1) * TOK] = gate_ref[...].astype(F32)
        grads[z * TOK : (z + 1) * TOK, :] = grad_ref[:, z * (X * LANES) : (z + 1) * (X * LANES)]
    step = 8 * BLOCK

    def body(i, carry):
        row = lax.broadcasted_iota(I32, (step, ZL * TOK), 0) + i * step
        take = jnp.where(row == keys[...], gates[...], 0.0).astype(BF16)
        out = jnp.dot(take, grads[...], preferred_element_type=F32).astype(BF16)
        for q in range(X):
            rows_ref[q, pl.ds(pl.multiple_of(i * step, step), step), :] = out[:, q * LANES : (q + 1) * LANES]
        return carry

    lax.fori_loop(0, E * BLOCK // step, body, 0)


def pack(ids, gates, grad):
    return pl.pallas_call(
        pack_kernel,
        out_shape=jax.ShapeDtypeStruct((X, E * BLOCK, LANES), BF16),
        scratch_shapes=[
            pltpu.VMEM((1, ZL * TOK), I32),
            pltpu.VMEM((1, ZL * TOK), F32),
            pltpu.VMEM((ZL * TOK, X * LANES), BF16),
        ],
        compiler_params=pltpu.CompilerParams(vmem_limit_bytes=VMEM),
        cost_estimate=pl.CostEstimate(flops=2 * E * BLOCK * ZL * TOK * X * LANES, bytes_accessed=3 << 20, transcendentals=0),
        name="pack",
    )(ids, gates, grad)


def weight_kernel(own_ref, recv_ref, acts_ref, *outs):
    parts, scaled_ref = outs[:ZB], outs[ZB]
    size = SUB * BLOCK
    group = SUB * CAP
    out = lax.broadcasted_iota(I32, (size, size), 0)
    col = lax.broadcasted_iota(I32, (size, size), 1)
    inner = out % group
    source = (inner // CAP) * BLOCK + (out // group) * CAP + inner % CAP
    order = jnp.where(source == col, 1.0, 0.0).astype(BF16)
    for k in range(FAN // SUB):
        rows = jnp.dot(order, recv_ref[k], preferred_element_type=F32).astype(BF16)
        for z in range(ZL):
            at = ((z % ZB) * ZA + z // ZB) * LANES
            scaled_ref[k * group : (k + 1) * group, at : at + LANES] = rows[z * group : (z + 1) * group, :]
    for d in range(ZB):
        at = pl.multiple_of(lax.rem(own_ref[0] + d, ZB) * (ZA * LANES), ZA * LANES)
        parts[d][...] = lax.dot_general(
            scaled_ref[:, pl.ds(at, ZA * LANES)],
            acts_ref[...],
            (((0,), (0,)), ((), ())),
            preferred_element_type=F32,
        ).astype(BF16)


def weight_part(own, recv, acts):
    vmem = pl.BlockSpec(memory_space=pltpu.VMEM)
    return pl.pallas_call(
        weight_kernel,
        in_specs=[pl.BlockSpec(memory_space=pltpu.SMEM), vmem, vmem],
        out_shape=[jax.ShapeDtypeStruct((ZA * LANES, FFW), BF16)] * ZB
        + [jax.ShapeDtypeStruct((ROWS, WIDE), BF16)],
        compiler_params=pltpu.CompilerParams(vmem_limit_bytes=VMEM),
        cost_estimate=pl.CostEstimate(flops=4 * ROWS * ROWS * WIDE, bytes_accessed=6 << 20, transcendentals=0),
        name="weight_part",
    )(own, recv, acts)


def act_kernel(own_ref, scaled_ref, weight_ref, acts_ref, *outs):
    parts, score_ref, grad = outs[:X], outs[X], outs[X + 1]
    grad[...] = jnp.dot(scaled_ref[...], weight_ref[...], preferred_element_type=F32)
    for d in range(X):
        at = pl.multiple_of(lax.rem(own_ref[0] + d, X) * SLOTS, SLOTS)
        parts[d][...] = grad[pl.ds(at, SLOTS), :].astype(BF16)
    narrow = jnp.zeros((ROWS, LANES), F32)
    for f in range(0, FFW, LANES):
        narrow = narrow + grad[:, f : f + LANES] * acts_ref[:, f : f + LANES].astype(F32)
    score_ref[...] = jnp.sum(narrow.T, axis=0, keepdims=True)


def act_part(own, scaled, weight, acts):
    vmem = pl.BlockSpec(memory_space=pltpu.VMEM)
    return pl.pallas_call(
        act_kernel,
        in_specs=[pl.BlockSpec(memory_space=pltpu.SMEM), vmem, vmem, vmem],
        out_shape=[jax.ShapeDtypeStruct((SLOTS, FFW), BF16)] * X + [jax.ShapeDtypeStruct((1, ROWS), F32)],
        scratch_shapes=[pltpu.VMEM((ROWS, FFW), F32)],
        compiler_params=pltpu.CompilerParams(vmem_limit_bytes=VMEM),
        cost_estimate=pl.CostEstimate(flops=2 * ROWS * FFW * WIDE, bytes_accessed=6 << 20, transcendentals=0),
        name="act_part",
    )(own, scaled, weight, acts)


def shift(block, axis, n, d):
    return lax.ppermute(block, axis, [(i, (i + d) % n) for i in range(n)])


def per_device(out_grad, expert_ids, gate_values, down_weight, gate_up):
    own_x, own_za, own_zb = (lax.axis_index(a) for a in ("x", "za", "zb"))
    rows = pack(expert_ids.reshape(1, TOK), gate_values.reshape(1, TOK), out_grad)
    recv = lax.all_to_all(
        rows.reshape(FAN, BLOCK, LANES), ("x",) + EXPERT, split_axis=0, concat_axis=0, tiled=True
    )

    saved = gate_up[0, 0]
    gate_act = saved[:, :FFW].astype(F32)
    up_act = saved[:, FFW:].astype(F32)
    sigmoid_val = jax.nn.sigmoid(gate_act)
    silu_val = gate_act * sigmoid_val
    hidden = (silu_val * up_act).astype(BF16)
    weight = lax.dynamic_index_in_dim(down_weight.reshape(ZA, ZB, X, LANES, FFW), own_x, 2, keepdims=False)
    weight = weight.swapaxes(0, 1).reshape(WIDE, FFW)
    chosen = expert_ids.reshape(TOK)
    onehot = (chosen[:, None] == jnp.arange(E, dtype=I32)[None, :]).astype(F32)
    later = jnp.arange(TOK)[:, None] > jnp.arange(TOK)[None, :]
    before = jnp.dot(later.astype(BF16), onehot.astype(BF16), preferred_element_type=F32)
    slots = chosen * CAP + jnp.sum(before * onehot, axis=1).astype(I32)
    hidden, weight, slots = lax.optimization_barrier((hidden, weight, slots))
    came = [hidden] + [shift(hidden, "x", X, d) for d in range(1, X)]
    turned = [came[-k % X] for k in range(X)]
    acts = lax.dynamic_slice_in_dim(jnp.concatenate(turned + turned), (X - own_x) % X * SLOTS, ROWS, 0)

    *sums, scaled = weight_part(own_zb.reshape(1), recv.reshape(FAN // SUB, SUB * BLOCK, LANES), acts)
    near = [sums[0]] + [shift(sums[d], "zb", ZB, d) for d in range(1, ZB)]
    *parts, score = act_part(own_x.reshape(1), scaled, weight, acts)
    near[1], parts, score = lax.optimization_barrier((near[1], parts, score))

    near = sum(part.astype(F32) for part in near)
    near = near.reshape(ZA, LANES, FFW)
    away = lax.dynamic_index_in_dim(near, 1 - own_za, 0, keepdims=False).astype(BF16)
    stay = lax.dynamic_index_in_dim(near, own_za, 0, keepdims=False)
    weight_share = (stay + shift(away, "za", ZA, 1).astype(F32)).astype(BF16)

    returned = lax.all_to_all(
        score.reshape(FAN, 1, CAP), ("x",) + EXPERT, split_axis=0, concat_axis=0, tiled=True
    )
    hidden_grad = parts[0].astype(F32)
    for d in range(1, X):
        hidden_grad = hidden_grad + shift(parts[d], "x", X, d).astype(F32)
    gate_part = hidden_grad * up_act * sigmoid_val * (1.0 + gate_act * (1.0 - sigmoid_val))
    up_part = hidden_grad * silu_val
    gu_grad = jnp.concatenate([gate_part, up_part], axis=1).astype(BF16)

    returned = jnp.sum(returned.reshape(X, SLOTS), axis=0)
    hit = slots[:, None] == jnp.arange(SLOTS, dtype=I32)[None, :]
    route = jnp.sum(jnp.where(hit, returned[None, :], 0.0), axis=1)
    route_grad = route.reshape(TOK, 1) / gate_values.astype(F32)
    return (weight_share[None], gu_grad[None, None], route_grad)


def solution(mesh):
    fine = Mesh(mesh.devices.reshape(ZA, ZB, X, ZH, Y, C), ("za", "zb", "x", "zh", "y", "c"))
    dp = ("za", "zb", "x")
    return jax.shard_map(
        per_device,
        mesh=fine,
        in_specs=(
            P(dp + EXPERT, None),
            P(dp + EXPERT, None),
            P(dp + EXPERT, None),
            P(EXPERT, None, None),
            P(dp, EXPERT, None, None),
        ),
        out_specs=(
            P(EXPERT, dp, None),
            P(dp, EXPERT, None, None),
            P(dp + EXPERT, None),
        ),
        check_vma=False,
    )
```

```python
import jax
import jax.numpy as jnp
from jax import lax
from jax.experimental import pallas as pl
from jax.experimental.pallas import tpu as pltpu
from jax.sharding import Mesh
from jax.sharding import PartitionSpec as P

BF16, F32, I32 = jnp.bfloat16, jnp.float32, jnp.int32
ZA, ZB, X, ZH, Y, C = 2, 4, 4, 4, 4, 2
ZL = ZA * ZB
E = ZH * Y * C
CAP = 6
TOK = 128
FFW = 768
LANES = 128
EXPERT = ("zh", "y", "c")
BLOCK = ZB * CAP
FAN = X * E
SLOTS = E * CAP
ROWS = X * SLOTS
WIDE = ZB * LANES
SUB = 16
VMEM = 24 * 1024 * 1024


def pack_kernel(ids_ref, gate_ref, grad_ref, low_ref, high_ref, keys, gates, grads):
    ids = ids_ref[...]
    onehot = (lax.broadcasted_iota(I32, (E, TOK), 0) == ids).astype(F32)
    earlier = lax.broadcasted_iota(I32, (TOK, TOK), 0) < lax.broadcasted_iota(I32, (TOK, TOK), 1)
    before = jnp.dot(onehot.astype(BF16), earlier.astype(BF16), preferred_element_type=F32)
    place = jnp.sum(before * onehot, axis=0, keepdims=True).astype(I32)
    base = ids * BLOCK + place
    for z in range(ZB):
        keys[:, z * TOK : (z + 1) * TOK] = base + z * CAP
        gates[:, z * TOK : (z + 1) * TOK] = gate_ref[...].astype(F32)
    for z in range(ZL):
        grads[z * TOK : (z + 1) * TOK, :] = grad_ref[:, z * (X * LANES) : (z + 1) * (X * LANES)]
    step = 8 * BLOCK
    deep = ZB * TOK

    def body(i, carry):
        row = lax.broadcasted_iota(I32, (step, deep), 0) + i * step
        take = jnp.where(row == keys[...], gates[...], 0.0).astype(BF16)
        for h, rows_ref in enumerate((low_ref, high_ref)):
            out = jnp.dot(take, grads[h * deep : (h + 1) * deep, :], preferred_element_type=F32).astype(BF16)
            for q in range(X):
                rows_ref[q, pl.ds(pl.multiple_of(i * step, step), step), :] = out[:, q * LANES : (q + 1) * LANES]
        return carry

    lax.fori_loop(0, E * BLOCK // step, body, 0)


def pack(ids, gates, grad):
    return pl.pallas_call(
        pack_kernel,
        out_shape=[jax.ShapeDtypeStruct((X, E * BLOCK, LANES), BF16)] * ZA,
        scratch_shapes=[
            pltpu.VMEM((1, ZB * TOK), I32),
            pltpu.VMEM((1, ZB * TOK), F32),
            pltpu.VMEM((ZL * TOK, X * LANES), BF16),
        ],
        compiler_params=pltpu.CompilerParams(vmem_limit_bytes=VMEM),
        cost_estimate=pl.CostEstimate(flops=4 * E * BLOCK * ZB * TOK * X * LANES, bytes_accessed=3 << 20, transcendentals=0),
        name="pack",
    )(ids, gates, grad)


def weight_kernel(own_ref, recv_ref, acts_ref, *outs):
    parts, scaled_ref, product = outs[:ZB], outs[ZB], outs[ZB + 1]
    size = SUB * BLOCK
    group = SUB * CAP
    out = lax.broadcasted_iota(I32, (size, size), 0)
    col = lax.broadcasted_iota(I32, (size, size), 1)
    inner = out % group
    source = (inner // CAP) * BLOCK + (out // group) * CAP + inner % CAP
    order = jnp.where(source == col, 1.0, 0.0).astype(BF16)
    for k in range(FAN // SUB):
        rows = jnp.dot(order, recv_ref[k], preferred_element_type=F32).astype(BF16)
        for z in range(ZB):
            scaled_ref[k * group : (k + 1) * group, z * LANES : (z + 1) * LANES] = rows[z * group : (z + 1) * group, :]
    product[...] = lax.dot_general(
        scaled_ref[...], acts_ref[...], (((0,), (0,)), ((), ())), preferred_element_type=F32
    )
    for d in range(ZB):
        at = pl.multiple_of(lax.rem(own_ref[0] + d, ZB) * LANES, LANES)
        parts[d][...] = product[pl.ds(at, LANES), :].astype(BF16)


def weight_part(own, recv, acts):
    vmem = pl.BlockSpec(memory_space=pltpu.VMEM)
    return pl.pallas_call(
        weight_kernel,
        in_specs=[pl.BlockSpec(memory_space=pltpu.SMEM), vmem, vmem],
        out_shape=[jax.ShapeDtypeStruct((LANES, FFW), BF16)] * ZB + [jax.ShapeDtypeStruct((ROWS, WIDE), BF16)],
        scratch_shapes=[pltpu.VMEM((WIDE, FFW), F32)],
        compiler_params=pltpu.CompilerParams(vmem_limit_bytes=VMEM),
        cost_estimate=pl.CostEstimate(flops=4 * ROWS * ROWS * WIDE, bytes_accessed=3 << 20, transcendentals=0),
        name="weight_part",
    )(own, recv.reshape(FAN // SUB, SUB * BLOCK, LANES), acts)


def act_kernel(own_ref, low_ref, high_ref, weight_ref, acts_ref, *outs):
    parts, score_ref, grad = outs[:X], outs[X], outs[X + 1]
    grad[...] = jnp.dot(low_ref[...], weight_ref[0], preferred_element_type=F32)
    grad[...] += jnp.dot(high_ref[...], weight_ref[1], preferred_element_type=F32)
    for d in range(X):
        at = pl.multiple_of(lax.rem(own_ref[0] + d, X) * SLOTS, SLOTS)
        parts[d][...] = grad[pl.ds(at, SLOTS), :].astype(BF16)
    narrow = jnp.zeros((ROWS, LANES), F32)
    for f in range(0, FFW, LANES):
        narrow = narrow + grad[:, f : f + LANES] * acts_ref[:, f : f + LANES].astype(F32)
    score_ref[...] = jnp.sum(narrow.T, axis=0, keepdims=True)


def act_part(own, low, high, weight, acts):
    vmem = pl.BlockSpec(memory_space=pltpu.VMEM)
    return pl.pallas_call(
        act_kernel,
        in_specs=[pl.BlockSpec(memory_space=pltpu.SMEM), vmem, vmem, vmem, vmem],
        out_shape=[jax.ShapeDtypeStruct((SLOTS, FFW), BF16)] * X + [jax.ShapeDtypeStruct((1, ROWS), F32)],
        scratch_shapes=[pltpu.VMEM((ROWS, FFW), F32)],
        compiler_params=pltpu.CompilerParams(vmem_limit_bytes=VMEM),
        cost_estimate=pl.CostEstimate(flops=4 * ROWS * FFW * WIDE, bytes_accessed=6 << 20, transcendentals=0),
        name="act_part",
    )(own, low, high, weight, acts)


def shift(block, axis, n, d):
    return lax.ppermute(block, axis, [(i, (i + d) % n) for i in range(n)])


def exchange(blocks):
    return lax.all_to_all(blocks, ("x",) + EXPERT, split_axis=0, concat_axis=0, tiled=True)


def per_device(out_grad, expert_ids, gate_values, down_weight, gate_up):
    own_x, own_za, own_zb = (lax.axis_index(a) for a in ("x", "za", "zb"))
    rows = pack(expert_ids.reshape(1, TOK), gate_values.reshape(1, TOK), out_grad)
    low = exchange(rows[0].reshape(FAN, BLOCK, LANES))

    saved = gate_up[0, 0]
    gate_act = saved[:, :FFW].astype(F32)
    up_act = saved[:, FFW:].astype(F32)
    sigmoid_val = jax.nn.sigmoid(gate_act)
    silu_val = gate_act * sigmoid_val
    hidden = (silu_val * up_act).astype(BF16)
    weight = lax.dynamic_index_in_dim(down_weight.reshape(ZL, X, LANES, FFW), own_x, 1, keepdims=False)
    weight = weight.reshape(ZA, WIDE, FFW)
    chosen = expert_ids.reshape(TOK)
    onehot = (chosen[:, None] == jnp.arange(E, dtype=I32)[None, :]).astype(F32)
    later = jnp.arange(TOK)[:, None] > jnp.arange(TOK)[None, :]
    before = jnp.dot(later.astype(BF16), onehot.astype(BF16), preferred_element_type=F32)
    slots = chosen * CAP + jnp.sum(before * onehot, axis=1).astype(I32)
    hidden, weight, slots = lax.optimization_barrier((hidden, weight, slots))
    came = [hidden] + [shift(hidden, "x", X, d) for d in range(1, X)]
    turned = [came[-k % X] for k in range(X)]
    acts = lax.dynamic_slice_in_dim(jnp.concatenate(turned + turned), (X - own_x) % X * SLOTS, ROWS, 0)

    low, behind, acts = lax.optimization_barrier((low, rows[1], acts))
    high = exchange(behind.reshape(FAN, BLOCK, LANES))
    own_zb = own_zb.reshape(1)
    *sums, scaled_low = weight_part(own_zb, low, acts)
    first = [sums[0]] + [shift(sums[d], "zb", ZB, d) for d in range(1, ZB)]
    high, first = lax.optimization_barrier((high, first))
    *sums, scaled_high = weight_part(own_zb, high, acts)
    second = [sums[0]] + [shift(sums[d], "zb", ZB, d) for d in range(1, ZB)]
    *parts, score = act_part(own_x.reshape(1), scaled_low, scaled_high, weight, acts)
    second[1], parts, score = lax.optimization_barrier((second[1], parts, score))
    near = jnp.stack([sum(part.astype(F32) for part in half) for half in (first, second)])
    away = lax.dynamic_index_in_dim(near, 1 - own_za, 0, keepdims=False).astype(BF16)
    stay = lax.dynamic_index_in_dim(near, own_za, 0, keepdims=False)
    weight_share = (stay + shift(away, "za", ZA, 1).astype(F32)).astype(BF16)

    returned = exchange(score.reshape(FAN, 1, CAP))
    hidden_grad = parts[0].astype(F32)
    for d in range(1, X):
        hidden_grad = hidden_grad + shift(parts[d], "x", X, d).astype(F32)
    gate_part = hidden_grad * up_act * sigmoid_val * (1.0 + gate_act * (1.0 - sigmoid_val))
    up_part = hidden_grad * silu_val
    gu_grad = jnp.concatenate([gate_part, up_part], axis=1).astype(BF16)

    returned = jnp.sum(returned.reshape(X, SLOTS), axis=0)
    hit = slots[:, None] == jnp.arange(SLOTS, dtype=I32)[None, :]
    route = jnp.sum(jnp.where(hit, returned[None, :], 0.0), axis=1)
    route_grad = route.reshape(TOK, 1) / gate_values.astype(F32)
    return (weight_share[None], gu_grad[None, None], route_grad)


def solution(mesh):
    fine = Mesh(mesh.devices.reshape(ZA, ZB, X, ZH, Y, C), ("za", "zb", "x", "zh", "y", "c"))
    dp = ("za", "zb", "x")
    return jax.shard_map(
        per_device,
        mesh=fine,
        in_specs=(
            P(dp + EXPERT, None),
            P(dp + EXPERT, None),
            P(dp + EXPERT, None),
            P(EXPERT, None, None),
            P(dp, EXPERT, None, None),
        ),
        out_specs=(
            P(EXPERT, dp, None),
            P(dp, EXPERT, None, None),
            P(dp + EXPERT, None),
        ),
        check_vma=False,
    )
```

```python
import jax
import jax.numpy as jnp
from jax import lax
from jax.experimental import pallas as pl
from jax.experimental.pallas import tpu as pltpu
from jax.sharding import Mesh
from jax.sharding import PartitionSpec as P

BF16, F32, I32 = jnp.bfloat16, jnp.float32, jnp.int32
ZA, ZB, X, ZH, Y, C = 2, 4, 4, 4, 4, 2
ZL = ZA * ZB
E = ZH * Y * C
CAP = 6
TOK = 128
FFW = 768
LANES = 128
EXPERT = ("zh", "y", "c")
BLOCK = ZL * CAP
FAN = X * E
SLOTS = E * CAP
ROWS = X * SLOTS
WIDE = ZL * LANES
SUB = 16
VMEM = 24 * 1024 * 1024


def pack_kernel(ids_ref, gate_ref, grad_ref, rows_ref, keys, gates, grads):
    ids = ids_ref[...]
    onehot = (lax.broadcasted_iota(I32, (E, TOK), 0) == ids).astype(F32)
    earlier = lax.broadcasted_iota(I32, (TOK, TOK), 0) < lax.broadcasted_iota(I32, (TOK, TOK), 1)
    before = jnp.dot(onehot.astype(BF16), earlier.astype(BF16), preferred_element_type=F32)
    place = jnp.sum(before * onehot, axis=0, keepdims=True).astype(I32)
    base = ids * BLOCK + place
    for z in range(ZL):
        keys[:, z * TOK : (z + 1) * TOK] = base + z * CAP
        gates[:, z * TOK : (z + 1) * TOK] = gate_ref[...].astype(F32)
        grads[z * TOK : (z + 1) * TOK, :] = grad_ref[:, z * (X * LANES) : (z + 1) * (X * LANES)]
    step = 8 * BLOCK

    def body(i, carry):
        row = lax.broadcasted_iota(I32, (step, ZL * TOK), 0) + i * step
        take = jnp.where(row == keys[...], gates[...], 0.0).astype(BF16)
        out = jnp.dot(take, grads[...], preferred_element_type=F32).astype(BF16)
        for q in range(X):
            rows_ref[q, pl.ds(pl.multiple_of(i * step, step), step), :] = out[:, q * LANES : (q + 1) * LANES]
        return carry

    lax.fori_loop(0, E * BLOCK // step, body, 0)


def pack(ids, gates, grad):
    return pl.pallas_call(
        pack_kernel,
        out_shape=jax.ShapeDtypeStruct((X, E * BLOCK, LANES), BF16),
        scratch_shapes=[
            pltpu.VMEM((1, ZL * TOK), I32),
            pltpu.VMEM((1, ZL * TOK), F32),
            pltpu.VMEM((ZL * TOK, X * LANES), BF16),
        ],
        compiler_params=pltpu.CompilerParams(vmem_limit_bytes=VMEM),
        cost_estimate=pl.CostEstimate(flops=2 * E * BLOCK * ZL * TOK * X * LANES, bytes_accessed=3 << 20, transcendentals=0),
        name="pack",
    )(ids, gates, grad)


def weight_kernel(own_ref, recv_ref, acts_ref, *outs):
    parts, scaled_ref = outs[:ZB], outs[ZB]
    size = SUB * BLOCK
    group = SUB * CAP
    out = lax.broadcasted_iota(I32, (size, size), 0)
    col = lax.broadcasted_iota(I32, (size, size), 1)
    inner = out % group
    source = (inner // CAP) * BLOCK + (out // group) * CAP + inner % CAP
    order = jnp.where(source == col, 1.0, 0.0).astype(BF16)
    for k in range(FAN // SUB):
        rows = jnp.dot(order, recv_ref[k], preferred_element_type=F32).astype(BF16)
        for z in range(ZL):
            at = ((z % ZB) * ZA + z // ZB) * LANES
            scaled_ref[k * group : (k + 1) * group, at : at + LANES] = rows[z * group : (z + 1) * group, :]
    for d in range(ZB):
        at = pl.multiple_of(lax.rem(own_ref[0] + d, ZB) * (ZA * LANES), ZA * LANES)
        parts[d][...] = lax.dot_general(
            scaled_ref[:, pl.ds(at, ZA * LANES)],
            acts_ref[...],
            (((0,), (0,)), ((), ())),
            preferred_element_type=F32,
        ).astype(BF16)


def weight_part(own, recv, acts):
    vmem = pl.BlockSpec(memory_space=pltpu.VMEM)
    return pl.pallas_call(
        weight_kernel,
        in_specs=[pl.BlockSpec(memory_space=pltpu.SMEM), vmem, vmem],
        out_shape=[jax.ShapeDtypeStruct((ZA * LANES, FFW), BF16)] * ZB
        + [jax.ShapeDtypeStruct((ROWS, WIDE), BF16)],
        compiler_params=pltpu.CompilerParams(vmem_limit_bytes=VMEM),
        cost_estimate=pl.CostEstimate(flops=4 * ROWS * ROWS * WIDE, bytes_accessed=6 << 20, transcendentals=0),
        name="weight_part",
    )(own, recv, acts)


def act_kernel(scaled_ref, weight_ref, acts_ref, *outs):
    part_ref, score_ref, grad = outs
    grad[...] = jnp.dot(scaled_ref[...], weight_ref[...], preferred_element_type=F32)
    part_ref[...] = grad[...].astype(BF16)
    narrow = jnp.zeros((ROWS, LANES), F32)
    for f in range(0, FFW, LANES):
        narrow = narrow + grad[:, f : f + LANES] * acts_ref[:, f : f + LANES].astype(F32)
    score_ref[...] = jnp.sum(narrow.T, axis=0, keepdims=True)


def act_part(scaled, weight, acts):
    vmem = pl.BlockSpec(memory_space=pltpu.VMEM)
    return pl.pallas_call(
        act_kernel,
        in_specs=[vmem, vmem, vmem],
        out_shape=[jax.ShapeDtypeStruct((ROWS, FFW), BF16)] + [jax.ShapeDtypeStruct((1, ROWS), F32)],
        scratch_shapes=[pltpu.VMEM((ROWS, FFW), F32)],
        compiler_params=pltpu.CompilerParams(vmem_limit_bytes=VMEM),
        cost_estimate=pl.CostEstimate(flops=2 * ROWS * FFW * WIDE, bytes_accessed=6 << 20, transcendentals=0),
        name="act_part",
    )(scaled, weight, acts)


def shift(block, axis, n, d):
    return lax.ppermute(block, axis, [(i, (i + d) % n) for i in range(n)])


def per_device(out_grad, expert_ids, gate_values, down_weight, gate_up):
    own_x, own_za, own_zb = (lax.axis_index(a) for a in ("x", "za", "zb"))
    rows = pack(expert_ids.reshape(1, TOK), gate_values.reshape(1, TOK), out_grad)
    recv = lax.all_to_all(
        rows.reshape(FAN, BLOCK, LANES), ("x",) + EXPERT, split_axis=0, concat_axis=0, tiled=True
    )

    saved = gate_up[0, 0]
    gate_act = saved[:, :FFW].astype(F32)
    up_act = saved[:, FFW:].astype(F32)
    sigmoid_val = jax.nn.sigmoid(gate_act)
    silu_val = gate_act * sigmoid_val
    hidden = (silu_val * up_act).astype(BF16)
    weight = lax.dynamic_index_in_dim(down_weight.reshape(ZA, ZB, X, LANES, FFW), own_x, 2, keepdims=False)
    weight = weight.swapaxes(0, 1).reshape(WIDE, FFW)
    chosen = expert_ids.reshape(TOK)
    onehot = (chosen[:, None] == jnp.arange(E, dtype=I32)[None, :]).astype(F32)
    later = jnp.arange(TOK)[:, None] > jnp.arange(TOK)[None, :]
    before = jnp.dot(later.astype(BF16), onehot.astype(BF16), preferred_element_type=F32)
    slots = chosen * CAP + jnp.sum(before * onehot, axis=1).astype(I32)
    hidden, weight, slots = lax.optimization_barrier((hidden, weight, slots))
    came = [hidden] + [shift(hidden, "x", X, d) for d in range(1, X)]
    turned = [came[-k % X] for k in range(X)]
    acts = lax.dynamic_slice_in_dim(jnp.concatenate(turned + turned), (X - own_x) % X * SLOTS, ROWS, 0)

    *sums, scaled = weight_part(own_zb.reshape(1), recv.reshape(FAN // SUB, SUB * BLOCK, LANES), acts)
    near = [sums[0]] + [shift(sums[d], "zb", ZB, d) for d in range(1, ZB)]
    *parts, score = act_part(scaled, weight, acts)
    raw, = parts
    raw_parts = lax.all_to_all(raw.reshape(X, SLOTS, FFW), "x", split_axis=0, concat_axis=0, tiled=True)
    near[1], raw_parts, score = lax.optimization_barrier((near[1], raw_parts, score))
    near = sum(part.astype(F32) for part in near)
    near = near.reshape(ZA, LANES, FFW)
    away = lax.dynamic_index_in_dim(near, 1 - own_za, 0, keepdims=False).astype(BF16)
    stay = lax.dynamic_index_in_dim(near, own_za, 0, keepdims=False)
    weight_share = (stay + shift(away, "za", ZA, 1).astype(F32)).astype(BF16)

    returned = lax.all_to_all(
        score.reshape(FAN, 1, CAP), ("x",) + EXPERT, split_axis=0, concat_axis=0, tiled=True
    )
    hidden_grad = jnp.sum(raw_parts.astype(F32), axis=0)
    gate_part = hidden_grad * up_act * sigmoid_val * (1.0 + gate_act * (1.0 - sigmoid_val))
    up_part = hidden_grad * silu_val
    gu_grad = jnp.concatenate([gate_part, up_part], axis=1).astype(BF16)

    returned = jnp.sum(returned.reshape(X, SLOTS), axis=0)
    hit = slots[:, None] == jnp.arange(SLOTS, dtype=I32)[None, :]
    route = jnp.sum(jnp.where(hit, returned[None, :], 0.0), axis=1)
    route_grad = route.reshape(TOK, 1) / gate_values.astype(F32)
    return (weight_share[None], gu_grad[None, None], route_grad)


def solution(mesh):
    fine = Mesh(mesh.devices.reshape(ZA, ZB, X, ZH, Y, C), ("za", "zb", "x", "zh", "y", "c"))
    dp = ("za", "zb", "x")
    return jax.shard_map(
        per_device,
        mesh=fine,
        in_specs=(
            P(dp + EXPERT, None),
            P(dp + EXPERT, None),
            P(dp + EXPERT, None),
            P(EXPERT, None, None),
            P(dp, EXPERT, None, None),
        ),
        out_specs=(
            P(EXPERT, dp, None),
            P(dp, EXPERT, None, None),
            P(dp + EXPERT, None),
        ),
        check_vma=False,
    )
```
